256 devices in a mesh: row: 16 (over x, y), col: 8 (over z), layer: 2 (over core).
Axes of the slice: x: 4, y: 4, z: 8, core: 2. Of those that a mesh axis runs over, the one named last changes fastest.
Arguments:
- initial: float32 [4096, 4096], P('row', 'col'), as said below
- occupancy: int32 [32, 32], replicated, may hold values from 0 to 1, as said below
Outputs:
- density: float32 [4096, 4096], P('row', 'col')
- occupation: float32 [], replicated
The draws below stay inside these ranges and needn't reach their ends.
Inputs may be any that keep to these rules, and one draw needn't show every extreme that they name: `initial`: symmetric. `occupancy`: symmetric; every diagonal block is kept.
All inputs are finite; a program needn't handle non-finite values.
Results may differ from the reference program's by a relative error of at most 0.0003.
Values sent between devices are 32-bit elements; how exact they have to be, the bound alone decides.
No kernel may reach another device: no remote copies, remote signals or barrier semaphores. Data moves between devices by JAX's collectives and lax.ppermute only.
A program may use at most 64 MiB of HBM per device.

```python
import jax
import jax.numpy as jnp
from jax import lax

BS = 128
ITERS = 2
NB = 32


def draw_initial(key, part):
    key = jax.random.fold_in(key, 11)
    noise_key, level_key = jax.random.split(key)
    order = NB * BS
    raw_noise = jax.random.normal(noise_key, (order, order), jnp.float32)
    low_end, rise = (0.15, 0.7)
    symmetric_noise = (raw_noise + raw_noise.T) * (0.004 / 1.4142)
    position = jnp.arange(order, dtype=jnp.float32) / order
    diagonal_level = (low_end + rise * position) * jax.random.uniform(level_key, (order,), jnp.float32, 0.8, 1.2)
    identity = jnp.eye(order, dtype=jnp.float32)
    return symmetric_noise * (1.0 - identity) + identity * diagonal_level[:, None]


def draw_occupancy(key, part):
    key = jax.random.fold_in(key, 23)
    reach = max(NB // 4, 1)
    far_reach = max(NB // 16, 1)
    kept_bits = (jax.random.randint(key, (NB, NB), 0, 4) != 0).astype(jnp.int32)
    index_row = jnp.arange(NB, dtype=jnp.int32)[:, None]
    index_col = jnp.arange(NB, dtype=jnp.int32)[None, :]
    near_band = (jnp.abs(index_row - index_col) <= reach).astype(jnp.int32)
    offset = jnp.mod(index_row - index_col, NB)
    far_gap = jnp.abs(offset - NB // 2)
    far_band = (far_gap <= far_reach).astype(jnp.int32)
    far_exact = (far_gap == 0).astype(jnp.int32)
    chosen = jnp.maximum(kept_bits * jnp.maximum(near_band, far_band), far_exact)
    upper_bits = jnp.triu(chosen, 1)
    occupied = upper_bits + upper_bits.T + jnp.eye(NB, dtype=jnp.int32)
    return jnp.minimum(occupied, 1).astype(jnp.int32)


def setup_inputs(seed: int = 0) -> dict:
    splits = jax.random.split(jax.random.key(seed), 3)
    initial = draw_initial(jax.random.fold_in(splits[2], 71), 0)
    occupancy = draw_occupancy(jax.random.fold_in(splits[2], 71), 0)
    return dict(initial=initial, occupancy=occupancy)


def expand(occupancy):
    blocks = occupancy.astype(jnp.float32)
    return jnp.repeat(jnp.repeat(blocks, BS, axis=0), BS, axis=1)


def product(left, right):
    return jnp.dot(left, right, precision=lax.Precision.HIGHEST, preferred_element_type=jnp.float32)


def reference(initial, occupancy):
    element_mask = expand(occupancy)
    density = initial * element_mask
    for iteration in range(ITERS):
        square = product(density, density)
        cube_term = product(density, square)
        density = (3.0 * square - 2.0 * cube_term) * element_mask
    occupation = jnp.sum(jnp.diagonal(density)) / (NB * BS)
    return density, occupation
```

```python
import jax
import jax.numpy as jnp
from jax import lax
from jax.sharding import PartitionSpec as P

BS = 128
ITERS = 2
NX, NY, NZ = 4, 4, 8


def product(left, right):
    return jnp.dot(left, right, precision=lax.Precision.HIGH, preferred_element_type=jnp.float32)


def z_shift(piece, step):
    return lax.ppermute(piece, "col", [(i, (i + step) % NZ) for i in range(NZ)])


def x_shift(piece, step):
    pairs = [(x * NY + y, (x + step) % NX * NY + y) for x in range(NX) for y in range(NY)]
    return lax.ppermute(piece, "row", pairs)


def y_shift(piece, step):
    pairs = [(x * NY + y, x * NY + (y + step) % NY) for x in range(NX) for y in range(NY)]
    return lax.ppermute(piece, "row", pairs)


def xor_total(value):
    for axis, size, bits in (("row", NX * NY, (4, 8, 1, 2)), ("col", NZ, (1, 2, 4))):
        for bit in bits:
            value = value + lax.ppermute(value, axis, [(i, i ^ bit) for i in range(size)])
    return value


def z_ring(piece):
    half = piece.shape[0] // 2
    after, before = [piece], [piece]
    for _ in range(3):
        after.append(z_shift(after[-1], -1))
        before.append(z_shift(before[-1], 1))
    far = jnp.concatenate([z_shift(after[3][:half], -1), z_shift(before[3][half:], 1)], axis=0)
    return after + [far] + before[:0:-1]


def ring_of_four(piece, shift):
    half = piece.shape[0] // 2
    after = shift(piece, -1)
    before = shift(piece, 1)
    far = jnp.concatenate([shift(after[:half], -1), shift(before[half:], 1)], axis=0)
    return after, far, before


def placed(pieces, first, axis):
    count = len(pieces)
    shape = list(pieces[0].shape)
    shape.insert(axis, count)
    stack = jnp.zeros(shape, pieces[0].dtype)
    for offset, piece in enumerate(pieces):
        stack = lax.dynamic_update_slice_in_dim(
            stack, jnp.expand_dims(piece, axis), lax.rem(first + offset, count), axis
        )
    return stack


def on_device(initial, occupancy):
    row = lax.axis_index("row")
    col = lax.axis_index("col")
    even = lax.axis_index("layer") == 0
    at_x, at_y = row // NY, lax.rem(row, NY)
    kept = lax.dynamic_slice(occupancy, (row * 2, col * 4), (2, 4))
    mask = jnp.concatenate(
        [
            jnp.concatenate(
                [jnp.broadcast_to(kept[i, j].astype(jnp.float32), (BS, BS)) for j in range(4)], axis=1
            )
            for i in range(2)
        ],
        axis=0,
    )

    def columns(matrix):
        return jnp.concatenate(
            [
                jnp.where(even, matrix[:, :BS], matrix[:, BS : 2 * BS]),
                jnp.where(even, matrix[:, 2 * BS : 3 * BS], matrix[:, 3 * BS :]),
            ],
            axis=1,
        )

    def rows(matrix):
        return jnp.where(even, matrix[:BS], matrix[BS:])

    def times_panel(pieces, left_panel, right_panel):
        total = [0.0, 0.0]
        for offset in (0, 1, 7, 2, 6, 3, 5, 4):
            at = lax.rem(col + offset, NZ)
            for side, panel in enumerate((left_panel, right_panel)):
                block = lax.dynamic_index_in_dim(panel, at, 0, keepdims=False)
                total[side] = total[side] + product(pieces[offset], block)
        total = jnp.concatenate(total, axis=1)
        return total + lax.ppermute(total, "layer", [(0, 1), (1, 0)])

    density = initial * mask
    for iteration in range(ITERS):
        with jax.named_scope("gather_panels"):
            mine = rows(density)
            along_x = ring_of_four(mine[:, : 2 * BS], x_shift)
            along_y = ring_of_four(mine[:, 2 * BS :], y_shift)
            row_pieces = z_ring(columns(density))
            along_x = placed((mine[:, : 2 * BS],) + along_x, at_x, 0)
            along_y = placed((mine[:, 2 * BS :],) + along_y, at_y, 0)
            left_panel = placed((along_x,) + ring_of_four(along_x, y_shift), at_y, 1)
            right_panel = placed((along_y,) + ring_of_four(along_y, x_shift), at_x, 0)
            left_panel = left_panel.reshape(NZ, 2 * BS, 2 * BS)
            right_panel = right_panel.reshape(NZ, 2 * BS, 2 * BS)
        with jax.named_scope("square"):
            square = times_panel(row_pieces, left_panel, right_panel)
        if iteration == ITERS - 1:
            with jax.named_scope("trace"):
                share = jnp.sum(density * (3.0 * density - 2.0 * square))
                occupation = xor_total(jnp.broadcast_to(share, (8, BS)))[0, 0]
        with jax.named_scope("cube"):
            cube_term = times_panel(z_ring(columns(square)), left_panel, right_panel)
        density = (3.0 * square - 2.0 * cube_term) * mask
    return density, occupation / (occupancy.shape[0] * BS)


def solution(mesh):
    placed = (P("row", "col"), P())
    return jax.shard_map(
        on_device, mesh=mesh, in_specs=placed, out_specs=(P("row", "col"), P()), check_vma=False
    )
```

```python
import jax
import jax.numpy as jnp
from jax import lax
from jax.sharding import PartitionSpec as P

BS = 128
ITERS = 2
NX, NY, NZ = 4, 4, 8
AXES = ("row", "col", "layer")


def product(left, right):
    return jnp.dot(left, right, precision=lax.Precision.HIGH, preferred_element_type=jnp.float32)


def index_of(x, y, z, core):
    return ((x % NX * NY + y % NY) * NZ + z % NZ) * 2 + core


def move(piece, steps):
    pairs = []
    for x in range(NX):
        for y in range(NY):
            for z in range(NZ):
                for core, (dx, dy, dz) in enumerate(steps):
                    pairs.append((index_of(x, y, z, core), index_of(x + dx, y + dy, z + dz, core)))
    return lax.ppermute(piece, AXES, pairs)


def swap_cores(piece):
    return lax.ppermute(piece, "layer", [(0, 1), (1, 0)])


def xor_total(value):
    for axis, size, bits in (("row", NX * NY, (4, 8, 1, 2)), ("col", NZ, (1, 2, 4))):
        for bit in bits:
            value = value + lax.ppermute(value, axis, [(i, i ^ bit) for i in range(size)])
    return value


def ring_of_four(piece, forward):
    backward = tuple(tuple(-step for step in steps) for steps in forward)
    half = piece.shape[0] // 2
    after = move(piece, backward)
    before = move(piece, forward)
    far = (move(after[:half], backward), move(before[half:], forward))
    stack = jnp.zeros((4,) + piece.shape, piece.dtype)
    stack = lax.dynamic_update_slice_in_dim(stack, piece[None], 0, 0)
    stack = lax.dynamic_update_slice_in_dim(stack, after[None], 1, 0)
    stack = lax.dynamic_update_slice_in_dim(stack, before[None], 3, 0)
    for place, part in ((0, far[0]), (half, far[1])):
        stack = lax.dynamic_update_slice(stack, part[None], (2, place) + (0,) * (piece.ndim - 1))
    return stack


def on_device(initial, occupancy):
    row = lax.axis_index("row")
    col = lax.axis_index("col")
    core = lax.axis_index("layer")
    even = core == 0
    way = 1 - 2 * core
    at_x, at_y = row // NY, lax.rem(row, NY)
    kept = lax.dynamic_slice(occupancy, (row * 2, col * 4), (2, 4))
    mask = jnp.concatenate(
        [
            jnp.concatenate(
                [jnp.broadcast_to(kept[i, j].astype(jnp.float32), (BS, BS)) for j in range(4)], axis=1
            )
            for i in range(2)
        ],
        axis=0,
    )

    def columns(matrix, first):
        return jnp.concatenate(
            [
                jnp.where(first, matrix[:, :BS], matrix[:, BS : 2 * BS]),
                jnp.where(first, matrix[:, 2 * BS : 3 * BS], matrix[:, 3 * BS :]),
            ],
            axis=1,
        )

    def rows(matrix):
        half = matrix.shape[0] // 2
        return jnp.where(even, matrix[:half], matrix[half:])

    def column_panel(matrix):
        once = ring_of_four(rows(matrix), ((1, 0, 0), (0, 1, 0)))
        return ring_of_four(once, ((0, 1, 0), (1, 0, 0))).reshape(NX * NY, BS, 4 * BS)

    def panel_block(panel, at):
        x = at // 2
        blocks = []
        for j in range(2):
            y = lax.rem(at, 2) * 2 + j
            off_x = lax.rem(x - at_x + NX, NX)
            off_y = lax.rem(y - at_y + NY, NY)
            place = jnp.where(even, off_y * NX + off_x, off_x * NY + off_y)
            blocks.append(lax.dynamic_index_in_dim(panel, place, 0, keepdims=False))
        return jnp.concatenate(blocks, axis=0)

    def row_pieces(matrix):
        yield 0, columns(matrix, even)
        held = matrix
        for step in range(1, 5):
            held = move(rows(held) if step == 4 else held, ((0, 0, -1), (0, 0, 1)))
            keep = columns(held, even)
            got = swap_cores(columns(held, ~even))
            if step < 4:
                yield way * step, keep
                yield -way * step, got
            else:
                yield 4, jnp.concatenate(
                    [jnp.where(even, keep, got), jnp.where(even, got, keep)], axis=0
                )

    def partial_product(matrix, panel):
        total = 0.0
        for offset, piece in row_pieces(matrix):
            total = total + product(piece, panel_block(panel, lax.rem(col + offset + NZ, NZ)))
        return total

    density = initial * mask
    for iteration in range(ITERS):
        with jax.named_scope("square"):
            panel = column_panel(density)
            part = partial_product(density, panel)
            square = part + swap_cores(part)
        if iteration == ITERS - 1:
            with jax.named_scope("trace"):
                share = jnp.sum(density * (1.5 * density - 2.0 * part))
                share = xor_total(jnp.broadcast_to(share, (8, 4 * BS)))
        with jax.named_scope("cube"):
            part = partial_product(square, panel)
            if iteration == ITERS - 1:
                part = jnp.concatenate([part, share], axis=0)
            cube_term = part + swap_cores(part)
        rows_here = initial.shape[0]
        if iteration == ITERS - 1:
            occupation = cube_term[rows_here, 0]
        density = (3.0 * square - 2.0 * cube_term[:rows_here]) * mask
    return density, occupation / (occupancy.shape[0] * BS)


def solution(mesh):
    placed = (P("row", "col"), P())
    return jax.shard_map(
        on_device, mesh=mesh, in_specs=placed, out_specs=(P("row", "col"), P()), check_vma=False
    )
```

```python
import jax
import jax.numpy as jnp
from jax import lax
from jax.sharding import PartitionSpec as P

BS = 128
ITERS = 2
NX, NY, NZ = 4, 4, 8
AXES = ("row", "col", "layer")


def product(left, right):
    return jnp.dot(left, right, precision=lax.Precision.HIGH, preferred_element_type=jnp.float32)


def index_of(x, y, z, core):
    return ((x % NX * NY + y % NY) * NZ + z % NZ) * 2 + core


def move(piece, steps):
    pairs = []
    for x in range(NX):
        for y in range(NY):
            for z in range(NZ):
                for core, (dx, dy, dz) in enumerate(steps):
                    pairs.append((index_of(x, y, z, core), index_of(x + dx, y + dy, z + dz, core)))
    return lax.ppermute(piece, AXES, pairs)


def swap_cores(piece):
    return lax.ppermute(piece, "layer", [(0, 1), (1, 0)])


def xor_total(value, hooks):
    inside = lax.axis_index("row") < NX * NY
    hooks = [None] + list(hooks)
    for axis, size, bits in (("row", NX * NY, (4, 8, 1, 2)), ("col", NZ, (1, 2, 4))):
        for bit in bits:
            hook = hooks.pop(0)
            if hook is not None:
                value = jnp.where(inside, value, hook[:8, :BS])
            value = value + lax.ppermute(value, axis, [(i, i ^ bit) for i in range(size)])
    return value


def ring_of_four(piece, forward):
    backward = tuple(tuple(-step for step in steps) for steps in forward)
    half = piece.shape[0] // 2
    after = move(piece, backward)
    before = move(piece, forward)
    far = (move(after[:half], backward), move(before[half:], forward))
    stack = jnp.zeros((4,) + piece.shape, piece.dtype)
    stack = lax.dynamic_update_slice_in_dim(stack, piece[None], 0, 0)
    stack = lax.dynamic_update_slice_in_dim(stack, after[None], 1, 0)
    stack = lax.dynamic_update_slice_in_dim(stack, before[None], 3, 0)
    for place, part in ((0, far[0]), (half, far[1])):
        stack = lax.dynamic_update_slice(stack, part[None], (2, place) + (0,) * (piece.ndim - 1))
    return stack


def on_device(initial, occupancy):
    row = lax.axis_index("row")
    col = lax.axis_index("col")
    core = lax.axis_index("layer")
    even = core == 0
    way = 1 - 2 * core
    at_x, at_y = row // NY, lax.rem(row, NY)
    row_block = lax.broadcasted_iota(jnp.int32, (2 * BS, NX * NY * 2), 0) // BS + row * 2
    col_block = lax.broadcasted_iota(jnp.int32, (NZ * 4, 4 * BS), 1) // BS + col * 4
    pick_rows = row_block == lax.broadcasted_iota(jnp.int32, row_block.shape, 1)
    pick_cols = col_block == lax.broadcasted_iota(jnp.int32, col_block.shape, 0)
    exact = jnp.bfloat16
    mask = jnp.dot(
        jnp.dot(pick_rows.astype(exact), occupancy.astype(exact)),
        pick_cols.astype(exact),
        preferred_element_type=jnp.float32,
    )

    def columns(matrix, first):
        return jnp.concatenate(
            [
                jnp.where(first, matrix[:, :BS], matrix[:, BS : 2 * BS]),
                jnp.where(first, matrix[:, 2 * BS : 3 * BS], matrix[:, 3 * BS :]),
            ],
            axis=1,
        )

    def rows(matrix):
        half = matrix.shape[0] // 2
        return jnp.where(even, matrix[:half], matrix[half:])

    def column_panel(matrix):
        once = ring_of_four(rows(matrix), ((1, 0, 0), (0, 1, 0)))
        return ring_of_four(once, ((0, 1, 0), (1, 0, 0))).reshape(NX * NY, BS, 4 * BS)

    def panel_block(panel, at):
        x = at // 2
        blocks = []
        for j in range(2):
            y = lax.rem(at, 2) * 2 + j
            off_x = lax.rem(x - at_x + NX, NX)
            off_y = lax.rem(y - at_y + NY, NY)
            place = jnp.where(even, off_y * NX + off_x, off_x * NY + off_y)
            blocks.append(lax.dynamic_index_in_dim(panel, place, 0, keepdims=False))
        return jnp.concatenate(blocks, axis=0)

    def partial_product(matrix, panel, share=None):
        total = 0.0

        def add(piece, offset):
            return total + product(piece, panel_block(panel, lax.rem(col + offset + NZ, NZ)))

        keep, give = columns(matrix, even), columns(matrix, ~even)
        total = add(keep, 0)
        hooks = []
        for step in range(1, 5):
            if step == 4:
                keep, give = rows(keep), rows(give)
            keep = move(keep, ((0, 0, -1), (0, 0, 1)))
            give = move(give, ((0, 0, -1), (0, 0, 1)))
            hooks += [keep, give]
            got = swap_cores(give)
            if step < 4:
                total = add(keep, way * step)
                total = add(got, -way * step)
            else:
                far = [jnp.where(even, keep, got), jnp.where(even, got, keep)]
                total = add(jnp.concatenate(far, axis=0), 4)
        if share is not None:
            share = xor_total(share, hooks)
        return total, share

    density = initial * mask
    for iteration in range(ITERS):
        last = iteration == ITERS - 1
        with jax.named_scope("square"):
            panel = column_panel(density)
            part, _ = partial_product(density, panel)
            square = part + swap_cores(part)
        with jax.named_scope("cube"):
            share = None
            if last:
                share = jnp.sum(density * (1.5 * density - 2.0 * part))
                share = jnp.broadcast_to(share, (8, BS))
            part, share = partial_product(square, panel, share)
            cube_term = part + swap_cores(part)
            if last:
                share = share + swap_cores(share)
                occupation = share[0, 0]
        density = (3.0 * square - 2.0 * cube_term) * mask
    return density, occupation / (occupancy.shape[0] * BS)


def solution(mesh):
    placed = (P("row", "col"), P())
    return jax.shard_map(
        on_device, mesh=mesh, in_specs=placed, out_specs=(P("row", "col"), P()), check_vma=False
    )
```

```python
import jax
import jax.numpy as jnp
from jax import lax
from jax.sharding import PartitionSpec as P

BS = 128
ITERS = 2
NX, NY, NZ = 4, 4, 8
AXES = ("row", "col", "layer")


def product(left, right):
    return jnp.dot(left, right, precision=lax.Precision.HIGH, preferred_element_type=jnp.float32)


def index_of(x, y, z, core):
    return ((x % NX * NY + y % NY) * NZ + z % NZ) * 2 + core


def move(piece, steps):
    pairs = []
    for x in range(NX):
        for y in range(NY):
            for z in range(NZ):
                for core, (dx, dy, dz) in enumerate(steps):
                    pairs.append((index_of(x, y, z, core), index_of(x + dx, y + dy, z + dz, core)))
    return lax.ppermute(piece, AXES, pairs)


def reverse(steps):
    return tuple(tuple(-step for step in one) for one in steps)


def swap_cores(piece):
    return lax.ppermute(piece, "layer", [(0, 1), (1, 0)])


def four_total(value, one, two):
    one, two = (one, one), (two, two)
    return (value + move(value, two)) + (move(value, one) + move(value, reverse(one)))


def on_device(initial, occupancy):
    row = lax.axis_index("row")
    col = lax.axis_index("col")
    core = lax.axis_index("layer")
    even = core == 0
    way = 1 - 2 * core
    inside = row < NX * NY
    at_x, at_y = row // NY, lax.rem(row, NY)
    row_block = lax.broadcasted_iota(jnp.int32, (2 * BS, NX * NY * 2), 0) // BS + row * 2
    col_block = lax.broadcasted_iota(jnp.int32, (NZ * 4, 4 * BS), 1) // BS + col * 4
    pick_rows = row_block == lax.broadcasted_iota(jnp.int32, row_block.shape, 1)
    pick_cols = col_block == lax.broadcasted_iota(jnp.int32, col_block.shape, 0)
    exact = jnp.bfloat16
    mask = jnp.dot(
        jnp.dot(pick_rows.astype(exact), occupancy.astype(exact)),
        pick_cols.astype(exact),
        preferred_element_type=jnp.float32,
    )

    def after(array, *others):
        tile = array[:8, :BS]
        for other in others:
            tile = jnp.where(inside, tile, other[:8, :BS])
        return lax.dynamic_update_slice(array, tile, (0, 0))

    def columns(matrix, first):
        return jnp.concatenate(
            [
                jnp.where(first, matrix[:, :BS], matrix[:, BS : 2 * BS]),
                jnp.where(first, matrix[:, 2 * BS : 3 * BS], matrix[:, 3 * BS :]),
            ],
            axis=1,
        )

    def rows(matrix):
        half = matrix.shape[0] // 2
        return jnp.where(even, matrix[:half], matrix[half:])

    def first_ring(matrix):
        one, two = ((1, 0, 0), (0, 1, 0)), ((2, 0, 0), (0, 2, 0))
        mine = rows(matrix)
        ring = (mine, move(mine, reverse(one)), move(mine, two), move(mine, one))
        return jnp.concatenate(ring, axis=0)

    def second_ring(stack):
        one = ((0, 1, 0), (1, 0, 0))
        half = stack.shape[0] // 2
        next_one, last_one = move(stack, reverse(one)), move(stack, one)
        far = move(next_one[:half], reverse(one)), move(last_one[half:], one)
        return stack, next_one, far[0], far[1], last_one

    def joined(parts):
        panel = jnp.zeros((NX * NY * BS, 4 * BS), jnp.float32)
        place = 0
        for part in parts:
            panel = lax.dynamic_update_slice_in_dim(panel, part, place, 0)
            place += part.shape[0]
        return panel.reshape(NX * NY, BS, 4 * BS)

    def panel_block(panel, at):
        x = at // 2
        blocks = []
        for j in range(2):
            y = lax.rem(at, 2) * 2 + j
            off_x = lax.rem(x - at_x + NX, NX)
            off_y = lax.rem(y - at_y + NY, NY)
            place = jnp.where(even, off_y * NX + off_x, off_x * NY + off_y)
            blocks.append(lax.dynamic_index_in_dim(panel, place, 0, keepdims=False))
        return jnp.concatenate(blocks, axis=0)

    def along_z(piece):
        return move(piece, ((0, 0, -1), (0, 0, 1)))

    def with_share(piece, share):
        return piece if share is None else jnp.concatenate([piece, share], axis=0)

    def partial_product(matrix, panel_of, share=None):
        size = matrix.shape[0]
        keep, give = columns(matrix, even), with_share(columns(matrix, ~even), share)
        pieces, shares = [(keep, 0)], [share]
        keep, give = along_z(keep), along_z(give)
        panel, waits = panel_of(keep, give)
        for step in range(1, 4):
            got = swap_cores(give)
            pieces += [(keep, way * step), (got[:size], -way * step)]
            shares += [give[size:], got[size:]]
            if step == 3:
                keep = rows(keep)
                give = with_share(rows(give[:size]), None if share is None else give[size:])
                if waits:
                    keep, give = after(keep, waits[0]), after(give, waits[1])
            keep, give = along_z(keep), along_z(give)
        shares.append(give[size // 2 :])
        got = swap_cores(give[: size // 2])
        far = [jnp.where(even, keep, got), jnp.where(even, got, keep)]
        pieces.append((jnp.concatenate(far, axis=0), 4))
        total = 0.0
        for piece, offset in pieces:
            total = total + product(piece, panel_block(panel, lax.rem(col + offset + NZ, NZ)))
        if share is not None:
            own, up1, down1, up2, down2, up3, down3, across = shares
            share = ((own + across) + (up2 + down2)) + ((up1 + down3) + (up3 + down1))
        return panel, total, share

    density = initial * mask
    for iteration in range(ITERS):
        last = iteration == ITERS - 1
        with jax.named_scope("square"):
            stack = first_ring(density)

            def gathered(keep, give):
                parts = second_ring(after(stack, keep, give))
                return joined(parts), (parts[1], parts[4])

            panel, part, _ = partial_product(density, gathered)
            square = part + swap_cores(part)
        with jax.named_scope("cube"):
            share = None
            if last:
                share = jnp.sum(density * (3.0 * density - 2.0 * square))
                share = jnp.broadcast_to(share, (8, 2 * BS))
            _, part, share = partial_product(square, lambda keep, give: (panel, ()), share)
            cube_term = part + swap_cores(part)
        density = (3.0 * square - 2.0 * cube_term) * mask
    with jax.named_scope("trace"):
        share = four_total(share[:, :BS], (1, 0, 0), (2, 0, 0))
        share = four_total(share, (0, 1, 0), (0, 2, 0))
        occupation = share[0, 0]
    return density, occupation / (occupancy.shape[0] * BS)


def solution(mesh):
    placed = (P("row", "col"), P())
    return jax.shard_map(
        on_device, mesh=mesh, in_specs=placed, out_specs=(P("row", "col"), P()), check_vma=False
    )
```

```python
import jax
import jax.numpy as jnp
from jax import lax
from jax.sharding import PartitionSpec as P

BS = 128
ITERS = 2
NX, NY, NZ = 4, 4, 8
AXES = ("row", "col", "layer")


def product(left, right):
    return jnp.dot(left, right, precision=lax.Precision.HIGH, preferred_element_type=jnp.float32)


def index_of(x, y, z, core):
    return ((x % NX * NY + y % NY) * NZ + z % NZ) * 2 + core


def move(piece, steps):
    pairs = []
    for x in range(NX):
        for y in range(NY):
            for z in range(NZ):
                for core, (dx, dy, dz) in enumerate(steps):
                    pairs.append((index_of(x, y, z, core), index_of(x + dx, y + dy, z + dz, core)))
    return lax.ppermute(piece, AXES, pairs)


def reverse(steps):
    return tuple(tuple(-step for step in one) for one in steps)


def swap_cores(piece):
    return lax.ppermute(piece, "layer", [(0, 1), (1, 0)])


def four_total(value, one, two):
    one, two = (one, one), (two, two)
    return (value + move(value, two)) + (move(value, one) + move(value, reverse(one)))


def on_device(initial, occupancy):
    row = lax.axis_index("row")
    col = lax.axis_index("col")
    core = lax.axis_index("layer")
    even = core == 0
    way = 1 - 2 * core
    inside = row < NX * NY
    at_x, at_y = row // NY, lax.rem(row, NY)
    row_block = lax.broadcasted_iota(jnp.int32, (2 * BS, NX * NY * 2), 0) // BS + row * 2
    col_block = lax.broadcasted_iota(jnp.int32, (NZ * 4, 4 * BS), 1) // BS + col * 4
    pick_rows = row_block == lax.broadcasted_iota(jnp.int32, row_block.shape, 1)
    pick_cols = col_block == lax.broadcasted_iota(jnp.int32, col_block.shape, 0)
    exact = jnp.bfloat16
    mask = jnp.dot(
        jnp.dot(pick_rows.astype(exact), occupancy.astype(exact)),
        pick_cols.astype(exact),
        preferred_element_type=jnp.float32,
    )

    def after(array, *others):
        tile = array[:8, :BS]
        for other in others:
            tile = jnp.where(inside, tile, other[:8, :BS])
        return lax.dynamic_update_slice(array, tile, (0, 0))

    def columns(matrix, first):
        return jnp.concatenate(
            [
                jnp.where(first, matrix[:, :BS], matrix[:, BS : 2 * BS]),
                jnp.where(first, matrix[:, 2 * BS : 3 * BS], matrix[:, 3 * BS :]),
            ],
            axis=1,
        )

    def rows(matrix):
        half = matrix.shape[0] // 2
        return jnp.where(even, matrix[:half], matrix[half:])

    def first_ring(matrix):
        one, two = ((1, 0, 0), (0, 1, 0)), ((2, 0, 0), (0, 2, 0))
        mine = rows(matrix)
        ring = (mine, move(mine, reverse(one)), move(mine, two), move(mine, one))
        return jnp.concatenate(ring[:2], axis=0), jnp.concatenate(ring[2:], axis=0)

    def second_ring(low, high):
        one = ((0, 1, 0), (1, 0, 0))
        low_next, high_last = move(low, reverse(one)), move(high, one)
        high_next, low_last = move(high, reverse(one)), move(low, one)
        low_far, high_far = move(low_next, reverse(one)), move(high_last, one)
        return low, high, low_next, high_next, low_far, high_far, low_last, high_last

    def joined(parts):
        panel = jnp.zeros((NX * NY * BS, 4 * BS), jnp.float32)
        place = 0
        for part in parts:
            panel = lax.dynamic_update_slice_in_dim(panel, part, place, 0)
            place += part.shape[0]
        return panel.reshape(NX * NY, BS, 4 * BS)

    def panel_block(panel, at):
        x = at // 2
        blocks = []
        for j in range(2):
            y = lax.rem(at, 2) * 2 + j
            off_x = lax.rem(x - at_x + NX, NX)
            off_y = lax.rem(y - at_y + NY, NY)
            place = jnp.where(even, off_y * NX + off_x, off_x * NY + off_y)
            blocks.append(lax.dynamic_index_in_dim(panel, place, 0, keepdims=False))
        return jnp.concatenate(blocks, axis=0)

    def along_z(piece):
        return move(piece, ((0, 0, -1), (0, 0, 1)))

    def with_share(piece, share):
        return piece if share is None else jnp.concatenate([piece, share], axis=0)

    def partial_product(matrix, panel_of, share=None):
        size = matrix.shape[0]
        keep, give = columns(matrix, even), with_share(columns(matrix, ~even), share)
        pieces, shares = [(keep, 0)], [share]
        give, keep = along_z(give), along_z(keep)
        panel, waits = panel_of(keep, give)
        for step in range(1, 4):
            got = swap_cores(give)
            pieces += [(keep, way * step), (got[:size], -way * step)]
            shares += [give[size:], got[size:]]
            if waits and step == 9:
                give, keep = after(give, waits[0][0]), after(keep, waits[0][1])
            if step == 3:
                keep = rows(keep)
                give = with_share(rows(give[:size]), None if share is None else give[size:])
                if waits:
                    give, keep = after(give, *waits[0]), after(keep, *waits[1])
            give, keep = along_z(give), along_z(keep)
        shares.append(give[size // 2 :])
        got = swap_cores(give[: size // 2])
        far = [jnp.where(even, keep, got), jnp.where(even, got, keep)]
        pieces.append((jnp.concatenate(far, axis=0), 4))
        total = 0.0
        for piece, offset in pieces:
            total = total + product(piece, panel_block(panel, lax.rem(col + offset + NZ, NZ)))
        if share is not None:
            own, up1, down1, up2, down2, up3, down3, across = shares
            share = ((own + across) + (up2 + down2)) + ((up1 + down3) + (up3 + down1))
        return panel, total, share

    density = initial * mask
    for iteration in range(ITERS):
        last = iteration == ITERS - 1
        with jax.named_scope("square"):
            low, high = first_ring(density)

            def gathered(keep, give):
                parts = second_ring(low, after(high, keep, give))
                return joined(parts), ((parts[2], parts[7]), (parts[3], parts[6]))

            panel, part, _ = partial_product(density, gathered)
            square = part + swap_cores(part)
        with jax.named_scope("cube"):
            share = None
            if last:
                share = jnp.sum(density * (3.0 * density - 2.0 * square))
                share = jnp.broadcast_to(share, (8, 2 * BS))
            _, part, share = partial_product(square, lambda keep, give: (panel, ()), share)
            cube_term = part + swap_cores(part)
        density = (3.0 * square - 2.0 * cube_term) * mask
    with jax.named_scope("trace"):
        share = four_total(share[:, :BS], (1, 0, 0), (2, 0, 0))
        share = four_total(share, (0, 1, 0), (0, 2, 0))
        occupation = share[0, 0]
    return density, occupation / (occupancy.shape[0] * BS)


def solution(mesh):
    placed = (P("row", "col"), P())
    return jax.shard_map(
        on_device, mesh=mesh, in_specs=placed, out_specs=(P("row", "col"), P()), check_vma=False
    )
```

```python
import jax
import jax.numpy as jnp
from jax import lax
from jax.sharding import PartitionSpec as P

BS = 128
ITERS = 2
NX, NY, NZ = 4, 4, 8
AXES = ("row", "col", "layer")


def product(left, right):
    return jnp.dot(left, right, precision=lax.Precision.HIGH, preferred_element_type=jnp.float32)


def index_of(x, y, z, core):
    return ((x % NX * NY + y % NY) * NZ + z % NZ) * 2 + core


def move(piece, steps):
    pairs = []
    for x in range(NX):
        for y in range(NY):
            for z in range(NZ):
                for core, (dx, dy, dz) in enumerate(steps):
                    pairs.append((index_of(x, y, z, core), index_of(x + dx, y + dy, z + dz, core)))
    return lax.ppermute(piece, AXES, pairs)


def reverse(steps):
    return tuple(tuple(-step for step in one) for one in steps)


def swap_cores(piece):
    return lax.ppermute(piece, "layer", [(0, 1), (1, 0)])


def four_total(value, one, two):
    one, two = (one, one), (two, two)
    return (value + move(value, two)) + (move(value, one) + move(value, reverse(one)))


def on_device(initial, occupancy):
    row = lax.axis_index("row")
    col = lax.axis_index("col")
    core = lax.axis_index("layer")
    even = core == 0
    way = 1 - 2 * core
    inside = row < NX * NY
    at_x, at_y = row // NY, lax.rem(row, NY)
    row_block = lax.broadcasted_iota(jnp.int32, (2 * BS, NX * NY * 2), 0) // BS + row * 2
    col_block = lax.broadcasted_iota(jnp.int32, (NZ * 4, 4 * BS), 1) // BS + col * 4
    pick_rows = row_block == lax.broadcasted_iota(jnp.int32, row_block.shape, 1)
    pick_cols = col_block == lax.broadcasted_iota(jnp.int32, col_block.shape, 0)
    exact = jnp.bfloat16
    mask = jnp.dot(
        jnp.dot(pick_rows.astype(exact), occupancy.astype(exact)),
        pick_cols.astype(exact),
        preferred_element_type=jnp.float32,
    )

    def after(array, *others):
        tile = array[:8, :BS]
        for other in others:
            tile = jnp.where(inside, tile, other[:8, :BS])
        return lax.dynamic_update_slice(array, tile, (0, 0))

    def columns(matrix, first):
        return jnp.concatenate(
            [
                jnp.where(first, matrix[:, :BS], matrix[:, BS : 2 * BS]),
                jnp.where(first, matrix[:, 2 * BS : 3 * BS], matrix[:, 3 * BS :]),
            ],
            axis=1,
        )

    def rows(matrix):
        half = matrix.shape[0] // 2
        return jnp.where(even, matrix[:half], matrix[half:])

    def first_ring(matrix):
        one, two = ((1, 0, 0), (0, 1, 0)), ((2, 0, 0), (0, 2, 0))
        mine = rows(matrix)
        ring = (mine, move(mine, reverse(one)), move(mine, two), move(mine, one))
        return jnp.concatenate(ring[:2], axis=0), jnp.concatenate(ring[2:], axis=0)

    def second_ring(low, high):
        one = ((0, 1, 0), (1, 0, 0))
        low_next, high_last = move(low, reverse(one)), move(high, one)
        high_next, low_last = move(high, reverse(one)), move(low, one)
        low_far, high_far = move(low_next, reverse(one)), move(high_last, one)
        return low, high, low_next, high_next, low_far, high_far, low_last, high_last

    def joined(parts):
        panel = jnp.zeros((NX * NY * BS, 4 * BS), jnp.float32)
        place = 0
        for part in parts:
            panel = lax.dynamic_update_slice_in_dim(panel, part, place, 0)
            place += part.shape[0]
        return panel.reshape(NX * NY, BS, 4 * BS)

    def panel_block(panel, at):
        x = at // 2
        blocks = []
        for j in range(2):
            y = lax.rem(at, 2) * 2 + j
            off_x = lax.rem(x - at_x + NX, NX)
            off_y = lax.rem(y - at_y + NY, NY)
            place = jnp.where(even, off_y * NX + off_x, off_x * NY + off_y)
            blocks.append(lax.dynamic_index_in_dim(panel, place, 0, keepdims=False))
        return jnp.concatenate(blocks, axis=0)

    def along_z(piece):
        return move(piece, ((0, 0, -1), (0, 0, 1)))

    def with_share(piece, share):
        return piece if share is None else jnp.concatenate([piece, share], axis=0)

    def partial_product(matrix, panel_of, share=None):
        size = matrix.shape[0]
        keep, give = columns(matrix, even), with_share(columns(matrix, ~even), share)
        pieces, shares = [(keep, 0)], [share]
        if share is not None:
            across = lax.ppermute(share, "col", [(i, (i + NZ // 2) % NZ) for i in range(NZ)])
        give, keep = along_z(give), along_z(keep)
        panel, waits = panel_of(keep, give)
        for step in range(1, 4):
            got = swap_cores(give)
            pieces += [(keep, way * step), (got[:size], -way * step)]
            shares += [give[size:], got[size:]]
            if waits and step == 9:
                give, keep = after(give, waits[0][0]), after(keep, waits[0][1])
            if step == 3:
                keep = rows(keep)
                give = rows(give[:size])
                if waits:
                    give, keep = after(give, *waits[0]), after(keep, *waits[1])
            give, keep = along_z(give), along_z(keep)
        if share is not None:
            own, up1, down1, up2, down2, up3, down3 = shares
            share = ((own + across) + (up2 + down2)) + ((up1 + down3) + (up3 + down1))
            share = four_total(share[:, :BS], (1, 0, 0), (2, 0, 0))
            give = after(give, share)
            share = four_total(share, (0, 1, 0), (0, 2, 0))
        got = swap_cores(give)
        far = [jnp.where(even, keep, got), jnp.where(even, got, keep)]
        far = jnp.concatenate(far, axis=0)
        pieces.append((far, 4))
        total = 0.0
        for piece, offset in pieces:
            total = total + product(piece, panel_block(panel, lax.rem(col + offset + NZ, NZ)))
        return panel, total, share

    density = initial * mask
    for iteration in range(ITERS):
        last = iteration == ITERS - 1
        with jax.named_scope("square"):
            low, high = first_ring(density)

            def gathered(keep, give):
                parts = second_ring(low, after(high, keep, give))
                return joined(parts), ((parts[2], parts[7]), (parts[3], parts[6]))

            panel, part, _ = partial_product(density, gathered)
            square = part + swap_cores(part)
        with jax.named_scope("cube"):
            share = None
            if last:
                share = jnp.sum(density * (3.0 * density - 2.0 * square))
                share = jnp.broadcast_to(share, (8, 2 * BS))
            _, part, share = partial_product(square, lambda keep, give: (panel, ()), share)
            cube_term = part + swap_cores(part)
        density = (3.0 * square - 2.0 * cube_term) * mask
    occupation = share[0, 0]
    return density, occupation / (occupancy.shape[0] * BS)


def solution(mesh):
    placed = (P("row", "col"), P())
    return jax.shard_map(
        on_device, mesh=mesh, in_specs=placed, out_specs=(P("row", "col"), P()), check_vma=False
    )
```

```python
import jax
import jax.numpy as jnp
from jax import lax
from jax.sharding import PartitionSpec as P

BS = 128
ITERS = 2
NX, NY, NZ = 4, 4, 8
AXES = ("row", "col", "layer")


def product(left, right):
    return jnp.dot(left, right, precision=lax.Precision.HIGH, preferred_element_type=jnp.float32)


def index_of(x, y, z, core):
    return ((x % NX * NY + y % NY) * NZ + z % NZ) * 2 + core


def move(piece, steps):
    pairs = []
    for x in range(NX):
        for y in range(NY):
            for z in range(NZ):
                for core, (dx, dy, dz) in enumerate(steps):
                    pairs.append((index_of(x, y, z, core), index_of(x + dx, y + dy, z + dz, core)))
    return lax.ppermute(piece, AXES, pairs)


def reverse(steps):
    return tuple(tuple(-step for step in one) for one in steps)


def swap_cores(piece):
    return lax.ppermute(piece, "layer", [(0, 1), (1, 0)])


def four_total(value, one, two):
    one, two = (one, one), (two, two)
    return (value + move(value, two)) + (move(value, one) + move(value, reverse(one)))


def on_device(initial, occupancy):
    row = lax.axis_index("row")
    col = lax.axis_index("col")
    core = lax.axis_index("layer")
    even = core == 0
    way = 1 - 2 * core
    inside = row < NX * NY
    at_x, at_y = row // NY, lax.rem(row, NY)
    row_block = lax.broadcasted_iota(jnp.int32, (2 * BS, NX * NY * 2), 0) // BS + row * 2
    col_block = lax.broadcasted_iota(jnp.int32, (NZ * 4, 4 * BS), 1) // BS + col * 4
    pick_rows = row_block == lax.broadcasted_iota(jnp.int32, row_block.shape, 1)
    pick_cols = col_block == lax.broadcasted_iota(jnp.int32, col_block.shape, 0)
    exact = jnp.bfloat16
    mask = jnp.dot(
        jnp.dot(pick_rows.astype(exact), occupancy.astype(exact)),
        pick_cols.astype(exact),
        preferred_element_type=jnp.float32,
    )

    def after(array, *others):
        tile = array[:8, :BS]
        for other in others:
            tile = jnp.where(inside, tile, other[:8, :BS])
        return lax.dynamic_update_slice(array, tile, (0, 0))

    def columns(matrix, first):
        return jnp.concatenate(
            [
                jnp.where(first, matrix[:, :BS], matrix[:, BS : 2 * BS]),
                jnp.where(first, matrix[:, 2 * BS : 3 * BS], matrix[:, 3 * BS :]),
            ],
            axis=1,
        )

    def rows(matrix):
        half = matrix.shape[0] // 2
        return jnp.where(even, matrix[:half], matrix[half:])

    def first_ring(matrix):
        one, two = ((1, 0, 0), (0, 1, 0)), ((2, 0, 0), (0, 2, 0))
        mine = rows(matrix)
        next_one, last_one = move(mine, reverse(one)), move(mine, one)
        ring = (mine, next_one, move(mine, two), last_one)
        return jnp.concatenate(ring[:2], axis=0), jnp.concatenate(ring[2:], axis=0)

    def second_ring(low, high):
        one = ((0, 1, 0), (1, 0, 0))
        low_next, high_last = move(low, reverse(one)), move(high, one)
        high_next, low_last = move(high, reverse(one)), move(low, one)
        low_far, high_far = move(low_next, reverse(one)), move(high_last, one)
        return low, high, low_next, high_next, low_far, high_far, low_last, high_last

    def joined(parts):
        panel = jnp.zeros((NX * NY * BS, 4 * BS), jnp.float32)
        place = 0
        for part in parts:
            panel = lax.dynamic_update_slice_in_dim(panel, part, place, 0)
            place += part.shape[0]
        return panel.reshape(NX * NY, BS, 4 * BS)

    def panel_block(panel, at):
        x = at // 2
        blocks = []
        for j in range(2):
            y = lax.rem(at, 2) * 2 + j
            off_x = lax.rem(x - at_x + NX, NX)
            off_y = lax.rem(y - at_y + NY, NY)
            place = jnp.where(even, off_y * NX + off_x, off_x * NY + off_y)
            blocks.append(lax.dynamic_index_in_dim(panel, place, 0, keepdims=False))
        return jnp.concatenate(blocks, axis=0)

    def along_z(piece):
        return move(piece, ((0, 0, -1), (0, 0, 1)))

    def with_share(piece, share):
        return piece if share is None else jnp.concatenate([piece, share], axis=0)

    def partial_product(matrix, panel_of, share=None):
        size = matrix.shape[0]
        keep, give = columns(matrix, even), with_share(columns(matrix, ~even), share)
        pieces, shares = [(keep, 0)], [share]
        if share is not None:
            across = lax.ppermute(share, "col", [(i, (i + NZ // 2) % NZ) for i in range(NZ)])
        give, keep = along_z(give), along_z(keep)
        panel, waits = panel_of(keep, give)
        for step in range(1, 4):
            got = swap_cores(give)
            pieces += [(keep, way * step), (got[:size], -way * step)]
            shares += [give[size:], got[size:]]
            if waits and step == 9:
                give, keep = after(give, waits[0][0]), after(keep, waits[0][1])
            if step == 3:
                keep = rows(keep)
                give = rows(give[:size])
                if waits:
                    give, keep = after(give, *waits[0]), after(keep, *waits[1])
            give, keep = along_z(give), along_z(keep)
        if share is not None:
            own, up1, down1, up2, down2, up3, down3 = shares
            share = ((own + across) + (up2 + down2)) + ((up1 + down3) + (up3 + down1))
            share = four_total(share[:, :BS], (1, 0, 0), (2, 0, 0))
            give = after(give, share)
            share = four_total(share, (0, 1, 0), (0, 2, 0))
        got = swap_cores(give)
        far = [jnp.where(even, keep, got), jnp.where(even, got, keep)]
        far = jnp.concatenate(far, axis=0)
        pieces.append((far, 4))
        total = 0.0
        for piece, offset in pieces:
            total = total + product(piece, panel_block(panel, lax.rem(col + offset + NZ, NZ)))
        return panel, total, share

    density = initial * mask
    for iteration in range(ITERS):
        last = iteration == ITERS - 1
        with jax.named_scope("square"):
            low, high = first_ring(density)

            def gathered(keep, give):
                parts = second_ring(low, after(high, keep, give))
                return joined(parts), ((parts[2], parts[7]), (parts[3], parts[6]))

            panel, part, _ = partial_product(density, gathered)
            square = part + swap_cores(part)
        with jax.named_scope("cube"):
            share = None
            if last:
                share = jnp.sum(density * (3.0 * density - 2.0 * square))
                share = jnp.broadcast_to(share, (8, 2 * BS))
            _, part, share = partial_product(square, lambda keep, give: (panel, ()), share)
            cube_term = part + swap_cores(part)
        density = (3.0 * square - 2.0 * cube_term) * mask
    occupation = after(share, density)[0, 0]
    return density, occupation / (occupancy.shape[0] * BS)


def solution(mesh):
    placed = (P("row", "col"), P())
    return jax.shard_map(
        on_device, mesh=mesh, in_specs=placed, out_specs=(P("row", "col"), P()), check_vma=False
    )
```
